256 devices in a mesh: dp: 8 (over z_lo, y), graph: 32 (over x, z_hi, core).
Axes of the slice: x: 4, y: 4, z: 8 (z_hi: 4, z_lo: 2; z = z_hi * 2 + z_lo), core: 2. Of those that a mesh axis runs over, the one named last changes fastest.
Arguments:
- node_embed: bfloat16 [8, 512, 1024], P('dp', 'graph'), may hold values from -6 to 6
- node_cotan: bfloat16 [8, 512, 1024], P('dp', 'graph'), may hold values from -6 to 6
- radial: bfloat16 [8, 24576, 128], P('dp', 'graph'), may hold values from -6 to 6
- source: int32 [8, 24576], P('dp', 'graph'), may hold values from 0 to 511
- target: int32 [8, 24576], P('dp', 'graph'), may hold values from 0 to 511
- edge_count: int32 [8, 32], P('dp', 'graph'), may hold values from 384 to 768, as said below
- w_source: bfloat16 [1024, 1024], replicated, may hold values from -0.1875 to 0.1875
- w_target: bfloat16 [1024, 1024], replicated, may hold values from -0.1875 to 0.1875
- w_out: bfloat16 [1024, 1024], replicated, may hold values from -0.1875 to 0.1875
- w_radial: bfloat16 [128, 1024], replicated, may hold values from -0.5 to 0.5
Outputs:
- node_grad: float32 [8, 512, 1024], P('dp', 'graph')
- grad_source: float32 [1024, 1024], P('graph')
- grad_target: float32 [1024, 1024], P('graph')
- grad_out: float32 [1024, 1024], P('graph')
- grad_radial: float32 [128, 1024], replicated
The draws below stay inside these ranges and needn't reach their ends.
Inputs may be any that keep to these rules, and one draw needn't show every extreme that they name: `edge_count`: edge slots of one graph index at or past its count are padding; in every batch one graph index has all 768 slots live.
All inputs are finite; a program needn't handle non-finite values.
Results may differ from the reference program's by a relative error of at most 0.019.
Values may be sent and summed in bfloat16 or wider, within the bound.
No kernel may reach another device: no remote copies, remote signals or barrier semaphores. Data moves between devices by JAX's collectives and lax.ppermute only.
A program may use at most 128 MiB of HBM per device.

```python
import jax
import jax.numpy as jnp
from jax import lax

D = 1024
RB = 128
EDGE_DEV = 768
NODES = 512
EDGES = 24576
N_DP = 8
N_GRAPH = 32


def draw_edge_count(key, part):
    key = jax.random.fold_in(key, 5)
    first, second = jax.random.split(key)
    base = jax.random.randint(first, (N_DP, N_GRAPH), EDGE_DEV // 2, EDGE_DEV + 1)
    picked = jax.random.randint(second, (N_DP, 1), 0, N_GRAPH)
    column = jnp.arange(N_GRAPH, dtype=jnp.int32)[None, :]
    return jnp.where(column == picked, EDGE_DEV, base).astype(jnp.int32)


def set_ends(drawn, rng, least, high):
    extent = drawn.shape
    place = [jax.random.randint(jax.random.fold_in(rng, axis), (), 0, extent[axis]) for axis in range(len(extent))]
    drawn = drawn.at[tuple(place)].set(least)
    longest = extent.index(max(extent))
    place[longest] = (place[longest] + 1) % extent[longest]
    return drawn.at[tuple(place)].set(high)


def level_of(own_key, dims, cuts, low, top_value):
    factor_of = 1.0
    for dim, blocks in cuts:
        draws = jax.random.uniform(jax.random.fold_in(jax.random.fold_in(own_key, 6), dim), (blocks,), jnp.float32, low / len(cuts), top_value / len(cuts))
        factor_of = factor_of * jnp.repeat(jnp.exp(draws), dims[dim] // blocks).reshape((-1,) + (1,) * (len(dims) - 1 - dim))
    return factor_of


def gaussian(rng, dims, scale, most, shards=(), held_as=jnp.bfloat16):
    result = scale * jax.random.normal(rng, dims, jnp.float32)
    if shards:
        result = result * level_of(rng, dims, shards, -0.22, 0.18)
    return jnp.clip(result, -most, most).astype(held_as)


def setup_inputs(seed: int = 0) -> dict:
    seeds = jax.random.split(jax.random.key(seed), 11)
    node_embed = gaussian(seeds[0], (N_DP, NODES, D), 1.0, 6.0, ((0, 8), (1, 32)))
    node_cotan = gaussian(seeds[1], (N_DP, NODES, D), 1.0, 6.0, ((0, 8), (1, 32)))
    radial = gaussian(seeds[2], (N_DP, EDGES, RB), 1.0, 6.0, ((0, 8), (1, 32)))
    source = set_ends(jax.random.randint(seeds[3], (N_DP, EDGES), 0, NODES), jax.random.fold_in(seeds[3], 1), 0, NODES - 1).astype(jnp.int32)
    target = set_ends(jax.random.randint(seeds[4], (N_DP, EDGES), 0, NODES), jax.random.fold_in(seeds[4], 1), 0, NODES - 1).astype(jnp.int32)
    edge_count = draw_edge_count(jax.random.fold_in(seeds[10], 71), 0)
    w_source = gaussian(seeds[6], (D, D), D ** -0.5, 0.1875)
    w_target = gaussian(seeds[7], (D, D), D ** -0.5, 0.1875)
    w_out = gaussian(seeds[8], (D, D), D ** -0.5, 0.1875)
    w_radial = gaussian(seeds[9], (RB, D), RB ** -0.5, 0.5)
    return {"node_embed": node_embed, "node_cotan": node_cotan, "radial": radial, "source": source, "target": target, "edge_count": edge_count, "w_source": w_source, "w_target": w_target, "w_out": w_out, "w_radial": w_radial}


def tdot(left, right):
    return lax.dot_general(left, right, (((0,), (0,)), ((), ())), preferred_element_type=jnp.float32)


def one_batch(embed, cotan, radial, source, target, count, w_source, w_target, w_out, w_radial):
    slots = jnp.arange(EDGES, dtype=jnp.int32)
    limit = jnp.repeat(count, EDGE_DEV)
    live = (slots % EDGE_DEV < limit).astype(jnp.float32)[:, None]
    hs = jnp.take(embed, source, axis=0)
    ht = jnp.take(embed, target, axis=0)
    gt = jnp.take(cotan, target, axis=0)
    pre = jnp.dot(hs, w_source, preferred_element_type=jnp.float32) + jnp.dot(ht, w_target, preferred_element_type=jnp.float32)
    rad = jnp.dot(radial, w_radial, preferred_element_type=jnp.float32)
    sig = jax.nn.sigmoid(pre)
    act = pre * sig
    message = (live * act * rad).astype(jnp.bfloat16)
    gmsg = live * lax.dot_general(gt, w_out, (((1,), (1,)), ((), ())), preferred_element_type=jnp.float32)
    grad_rad = (gmsg * act).astype(jnp.bfloat16)
    grad_pre = (gmsg * rad * sig * (1.0 + pre * (1.0 - sig))).astype(jnp.bfloat16)
    g_out = tdot(message, gt)
    g_source = tdot(hs, grad_pre)
    g_target = tdot(ht, grad_pre)
    g_radial = tdot(radial, grad_rad)
    push_source = lax.dot_general(grad_pre, w_source, (((1,), (1,)), ((), ())), preferred_element_type=jnp.float32).astype(jnp.bfloat16)
    push_target = lax.dot_general(grad_pre, w_target, (((1,), (1,)), ((), ())), preferred_element_type=jnp.float32).astype(jnp.bfloat16)
    node_sum = jax.ops.segment_sum(push_source.astype(jnp.float32), source, num_segments=NODES)
    node_sum = node_sum + jax.ops.segment_sum(push_target.astype(jnp.float32), target, num_segments=NODES)
    node_grad = cotan.astype(jnp.float32) + node_sum
    return node_grad, g_source, g_target, g_out, g_radial


def reference(node_embed, node_cotan, radial, source, target, edge_count, w_source, w_target, w_out, w_radial):
    def step(carry, items):
        embed, cotan, rad_in, src, tgt, count = items
        node_grad, g_source, g_target, g_out, g_radial = one_batch(embed, cotan, rad_in, src, tgt, count, w_source, w_target, w_out, w_radial)
        carry = (carry[0] + g_source, carry[1] + g_target, carry[2] + g_out, carry[3] + g_radial)
        return carry, node_grad

    start = (jnp.zeros((D, D), jnp.float32), jnp.zeros((D, D), jnp.float32), jnp.zeros((D, D), jnp.float32), jnp.zeros((RB, D), jnp.float32))
    totals, node_grad = lax.scan(step, start, (node_embed, node_cotan, radial, source, target, edge_count))
    return node_grad, totals[0], totals[1], totals[2], totals[3]
```

```python
import jax
import jax.numpy as jnp
from jax import lax
from jax.sharding import Mesh
from jax.sharding import PartitionSpec as P

BF = jnp.bfloat16
F32 = jnp.float32


def dot(left, right, dims=((1,), (0,))):
    return lax.dot_general(left, right, (dims, ((), ())), preferred_element_type=F32)


def pick(array, index, axis):
    return lax.dynamic_index_in_dim(array, index, axis, keepdims=False)


def send(array, axis, offset):
    size = lax.axis_size(axis)
    return lax.ppermute(array, axis, [(i, (i + offset) % size) for i in range(size)])


def gather_from(array, axis):
    return [array] + [send(array, axis, -o) for o in range(1, lax.axis_size(axis))]


def trade(pieces, axis):
    return [pieces[0]] + [send(pieces[o], axis, o) for o in range(1, len(pieces))]


def total(parts):
    out = parts[0].astype(F32)
    for part in parts[1:]:
        out = out + part.astype(F32)
    return out


def in_order(parts, me):
    size = len(parts)
    stacked = jnp.stack(parts)
    return jnp.stack([pick(stacked, (me - a) % size, 0) for a in range(size)])


def natural(array, lead):
    return array.reshape(lead, 4, 2, 4, 32).transpose(0, 1, 3, 2, 4).reshape(lead, 1024)


def gather_nodes(own):
    z = jnp.stack(gather_from(own, "zhi"))
    x = jnp.stack(gather_from(z, "x"))
    c = jnp.stack(gather_from(x, "core"))
    return c.transpose(2, 1, 0, 3, 4).reshape(512, 1024)


def per_device(
    node_embed, node_cotan, radial, source, target, edge_count, w_source, w_target, w_out, w_radial
):
    my_y, my_x = lax.axis_index("y"), lax.axis_index("x")
    my_z, my_c = lax.axis_index("zhi"), lax.axis_index("core")
    cotan = node_cotan[0]
    embed_all = gather_nodes(node_embed[0])
    cotan_all = gather_nodes(cotan)

    live = jnp.arange(768, dtype=jnp.int32) < edge_count[0, 0]
    ids = jnp.where(live[None], jnp.stack([source[0], target[0]]), -1).reshape(12, 128)
    ids = jnp.stack(gather_from(jnp.stack(gather_from(ids, "x")), "core"))
    ids = ids.reshape(8, 2, 768).transpose(1, 0, 2).reshape(2, 6144)
    rad_in = jnp.stack(gather_from(jnp.stack(gather_from(radial[0], "x")), "core")).reshape(6144, 128)
    n_x, n_z, n_c, n_r = ids >> 7, (ids >> 5) & 3, (ids >> 4) & 1, ids & 15
    place = (((n_z - my_z) & 3) * 8 + ((n_x - my_x) & 3) * 2 + (n_c ^ my_c)) * 16 + n_r
    place = jnp.where(ids >= 0, place, -1)
    wanted = jnp.arange(512, dtype=jnp.int32)
    hot_s = (place[0][:, None] == wanted[None]).astype(BF)
    hot_t = (place[1][:, None] == wanted[None]).astype(BF)

    lane = jnp.arange(128, dtype=jnp.int32)
    sel = (
        jnp.arange(256, dtype=jnp.int32)[:, None] == ((lane >> 5) * 64 + my_c * 32 + (lane & 31))[None]
    ).astype(BF)

    def columns(weight):
        part = lax.dynamic_slice_in_dim(weight, my_x * 256, 256, 1)
        return dot(part, sel).astype(BF)

    wo = lax.dynamic_slice_in_dim(w_out, my_x * 256, 256, 0).reshape(4, 2, 32, 1024)
    wo = pick(wo, my_c, 1).reshape(128, 1024)
    p_s = dot(embed_all, columns(w_source)).astype(BF)
    p_t = dot(embed_all, columns(w_target)).astype(BF)
    q = dot(cotan_all, wo, ((1,), (1,))).astype(BF)

    pre = dot(hot_s, p_s) + dot(hot_t, p_t)
    rad = dot(rad_in, columns(w_radial))
    sig = jax.nn.sigmoid(pre)
    act = pre * sig
    message = (act * rad).astype(BF)
    gmsg = dot(hot_t, q)
    grad_rad = (gmsg * act).astype(BF)
    grad_pre = (gmsg * rad * sig * (1.0 + pre * (1.0 - sig))).astype(BF)
    m_sum = dot(hot_t, message, ((0,), (0,))).astype(BF)
    s_src = dot(hot_s, grad_pre, ((0,), (0,))).astype(BF)
    s_tgt = dot(hot_t, grad_pre, ((0,), (0,))).astype(BF)
    g_rad = dot(rad_in, grad_rad, ((0,), (0,))).astype(BF)

    s_both = jnp.stack([s_src, s_tgt], 1).reshape(4, 4, 2, 16, 2, 128)
    s_both = total(trade([s_both[o] for o in range(4)], "zhi")).astype(BF)
    s_both = jnp.stack(trade([s_both[o] for o in range(4)], "x"))
    s_both = trade([s_both[:, 0], s_both[:, 1]], "core")
    s_both = jnp.stack([in_order([s[o] for o in range(4)], my_x) for s in s_both])
    s_both = jnp.stack([pick(s_both, my_c, 0), pick(s_both, 1 - my_c, 0)])
    s_own = natural(s_both.transpose(3, 2, 1, 0, 4).reshape(32, 4, 2, 128), 32).reshape(2, 16, 1024)
    node_grad = (
        cotan.astype(F32)
        + dot(s_own[0], w_source, ((1,), (1,)))
        + dot(s_own[1], w_target, ((1,), (1,)))
    )

    g_s = dot(embed_all, s_src, ((0,), (0,))).astype(BF).reshape(4, 4, 2, 4, 8, 128)
    g_t = dot(embed_all, s_tgt, ((0,), (0,))).astype(BF).reshape(4, 4, 2, 4, 8, 128)
    g_o = dot(m_sum, cotan_all, ((0,), (0,))).astype(BF).reshape(4, 4, 8, 8, 128)
    g_rad = g_rad.reshape(4, 32, 128)

    def y_piece(o):
        at = (my_y + o) & 3
        return jnp.concatenate(
            [
                pick(g_s, at, 3).reshape(256, 128),
                pick(g_t, at, 3).reshape(256, 128),
                pick(g_o, at, 1).reshape(256, 128),
                pick(g_rad, at, 0),
            ]
        )

    summed = total(trade([y_piece(o) for o in range(4)], "y")).astype(BF)
    w_st = summed[:512].reshape(2, 4, 4, 2, 8, 128)
    w_o = summed[512:768].reshape(4, 64, 128)
    w_r = summed[768:]

    def z_piece(o):
        at = (my_z + o) & 3
        return jnp.concatenate([pick(w_st, at, 2).reshape(128, 128), pick(w_o, at, 0), w_r])

    parts = trade([z_piece(o) for o in range(4)], "zhi")
    radial_part = total([in_order([p[192:] for p in parts], my_z)[a] for a in range(4)])
    summed = jnp.concatenate([total([p[:192] for p in parts]), radial_part]).astype(BF)
    summed = total(gather_from(summed, "zlo")).astype(BF)
    w_st = summed[:128].reshape(2, 4, 16, 128)
    w_o = summed[128:192].reshape(8, 8, 128)
    w_r = summed[192:]

    def x_piece(o):
        at = (my_x + o) & 3
        return jnp.concatenate([pick(w_st, at, 1).reshape(32, 128), w_r])

    parts = in_order(trade([x_piece(o) for o in range(4)], "x"), my_x)
    w_st, w_r = parts[:, :32].reshape(4, 2, 2, 8, 128), parts[:, 32:]

    def c_piece(at):
        return jnp.concatenate([pick(w_st, at, 2).reshape(4, 16, 128), w_r], 1)

    mine, other = trade([c_piece(my_c), c_piece(1 - my_c)], "core")
    both = jnp.stack([mine, other])
    both = jnp.stack([pick(both, my_c, 0), pick(both, 1 - my_c, 0)])
    rows = natural(both.transpose(2, 1, 0, 3).reshape(48, 4, 2, 128), 48)
    rows = jnp.concatenate([rows[:16], w_o.transpose(0, 1, 2).reshape(8, 1024), rows[16:]])
    rows = in_order(trade([rows] * 4, "y"), my_y).astype(F32)
    return (
        node_grad[None],
        rows[:, :8].reshape(32, 1024),
        rows[:, 8:16].reshape(32, 1024),
        rows[:, 16:24].reshape(32, 1024),
        rows[:, 24:].reshape(128, 1024),
    )


def solution(mesh):
    fine = Mesh(mesh.devices.reshape(2, 4, 4, 4, 2), ("zlo", "y", "x", "zhi", "core"))
    dp, graph = ("zlo", "y"), ("x", "zhi", "core")
    placed = (
        P(dp, graph, None),
        P(dp, graph, None),
        P(dp, graph, None),
        P(dp, graph),
        P(dp, graph),
        P(dp, graph),
        P(),
        P(),
        P(),
        P(),
    )
    return jax.shard_map(
        per_device,
        mesh=fine,
        in_specs=placed,
        out_specs=(
            P(dp, graph, None),
            P(graph, None),
            P(graph, None),
            P(graph, None),
            P(),
        ),
        check_vma=False,
    )
```

```python
import jax
import jax.numpy as jnp
from jax import lax
from jax.experimental import pallas as pl
from jax.experimental.pallas import tpu as pltpu
from jax.sharding import Mesh
from jax.sharding import PartitionSpec as P

BF = jnp.bfloat16
F32 = jnp.float32


def dot(left, right, dims=((1,), (0,))):
    return lax.dot_general(left, right, (dims, ((), ())), preferred_element_type=F32)


def pick(array, index, axis):
    return lax.dynamic_index_in_dim(array, index, axis, keepdims=False)


def send(array, axis, offset):
    size = lax.axis_size(axis)
    return lax.ppermute(array, axis, [(i, (i + offset) % size) for i in range(size)])


def gather_from(array, axis):
    return [array] + [send(array, axis, -o) for o in range(1, lax.axis_size(axis))]


def trade(pieces, axis):
    return [pieces[0]] + [send(pieces[o], axis, o) for o in range(1, len(pieces))]


def total(parts):
    out = parts[0].astype(F32)
    for part in parts[1:]:
        out = out + part.astype(F32)
    return out


def in_order(parts, me):
    size = len(parts)
    stacked = jnp.stack(parts)
    return jnp.stack([pick(stacked, (me - a) % size, 0) for a in range(size)])


def natural(array, lead):
    return array.reshape(lead, 4, 2, 4, 32).transpose(0, 1, 3, 2, 4).reshape(lead, 1024)


def edge_kernel(
    at_ref, mine_ref, sib_ref, ws_ref, wt_ref, wo_ref, wr_ref, edge_mine_ref, edge_sib_ref,
    sums_ref, grads_ref, embed, cotan, p_s, p_tq, acc_s, acc_t, acc_r
):
    step = pl.program_id(0)
    my_y, my_x, my_z, my_c = (at_ref[i] for i in range(4))

    @pl.when(step == 0)
    def _():
        for half, ref in enumerate((mine_ref, sib_ref)):
            rows = pl.ds(half * 256, 256)
            embed[rows] = ref[:, :, 0].reshape(256, 1024)
            cotan[rows] = ref[:, :, 1].reshape(256, 1024)
        p_s[...] = dot(embed[...], ws_ref[...]).T.astype(BF)
        p_tq[:128] = dot(embed[...], wt_ref[...]).T.astype(BF)
        p_tq[128:] = dot(wo_ref[...], cotan[...], ((1,), (1,))).astype(BF)
        acc_s[...] = jnp.zeros_like(acc_s)
        acc_t[...] = jnp.zeros_like(acc_t)
        acc_r[...] = jnp.zeros_like(acc_r)

    edges = jnp.where(step < 4, edge_mine_ref[0], edge_sib_ref[0])
    radial = edges[:768]
    coded = edges[768:].astype(F32)
    node = (coded[:12] * 16.0 + coded[12:24]).astype(jnp.int32) - 1
    far_z = ((node >> 5) - my_z) & 3
    far_x = ((node >> 7) - my_x) & 3
    far_c = ((node >> 4) & 1) ^ my_c
    place = (far_c * 16 + far_x * 4 + far_z) * 16 + (node & 15)
    place = jnp.where(node >= 0, place, -1)
    spot = lax.broadcasted_iota(jnp.int32, (512, 768), 0)

    def hot(first):
        row = jnp.concatenate([place[first + i : first + i + 1] for i in range(6)], axis=1)
        return (spot == row).astype(F32).astype(BF)

    hot_s, hot_t = hot(0), hot(6)
    both = dot(p_tq[...], hot_t)
    pre = dot(p_s[...], hot_s) + both[:128]
    gmsg = both[128:]
    rad = dot(wr_ref[...], radial, ((1,), (1,)))
    sig = 1.0 / (1.0 + jnp.exp(-pre))
    act = pre * sig
    message = (act * rad).astype(BF)
    grad_rad = (gmsg * act).astype(BF)
    grad_pre = (gmsg * rad * (sig + act * (1.0 - sig))).astype(BF)
    acc_t[...] += dot(jnp.concatenate([message, grad_pre]), hot_t, ((1,), (1,)))
    acc_s[...] += dot(grad_pre, hot_s, ((1,), (1,)))
    acc_r[...] += dot(grad_rad, radial)

    @pl.when(step == 7)
    def _():
        for mat, flat in enumerate((acc_s[...], acc_t[128:])):
            nodes = flat.T.astype(BF)
            for c in range(2):
                for x in range(4):
                    for z in range(4):
                        first = (c * 16 + x * 4 + z) * 16
                        sums_ref[z, x, c, mat] = nodes[first : first + 16]
            grad = dot(flat.astype(BF), embed[...]).T.astype(BF)
            for h in range(2):
                to = (2 * mat + h - my_y) & 3
                for i in range(32):
                    grads_ref[to, i * 16 : i * 16 + 16] = grad[i * 32 + h * 16 : i * 32 + h * 16 + 16]
        grad = dot(acc_t[:128].astype(BF), cotan[...]).astype(BF)
        for k in range(2):
            for h in range(2):
                to = (2 * k + h - my_y) & 3
                for z in range(4):
                    for b in range(4):
                        first, at = z * 32 + h * 16, 512 + (z * 4 + b) * 16
                        lanes = slice(k * 512 + b * 128, k * 512 + b * 128 + 128)
                        grads_ref[to, at : at + 16] = grad[first : first + 16, lanes]
        grad = acc_r[...].T.astype(BF)
        for y in range(4):
            grads_ref[(y - my_y) & 3, 768:800] = grad[y * 32 : y * 32 + 32]


def edge_pass(at, mine, sib, ws, wt, wo, wr, edge_mine, edge_sib):
    def whole(array):
        return pl.BlockSpec(array.shape, lambda i: (0,) * array.ndim)

    return pl.pallas_call(
        edge_kernel,
        grid=(8,),
        in_specs=[
            pl.BlockSpec(memory_space=pltpu.SMEM),
            whole(mine),
            whole(sib),
            whole(ws),
            whole(wt),
            whole(wo),
            whole(wr),
            pl.BlockSpec((1, 800, 128), lambda i: (jnp.minimum(i, 3), 0, 0)),
            pl.BlockSpec((1, 800, 128), lambda i: (jnp.maximum(i - 4, 0), 0, 0)),
        ],
        out_specs=[
            pl.BlockSpec((4, 4, 2, 2, 16, 128), lambda i: (0,) * 6),
            pl.BlockSpec((4, 800, 128), lambda i: (0,) * 3),
        ],
        out_shape=[
            jax.ShapeDtypeStruct((4, 4, 2, 2, 16, 128), BF),
            jax.ShapeDtypeStruct((4, 800, 128), BF),
        ],
        scratch_shapes=[
            pltpu.VMEM((512, 1024), BF),
            pltpu.VMEM((512, 1024), BF),
            pltpu.VMEM((128, 512), BF),
            pltpu.VMEM((256, 512), BF),
            pltpu.VMEM((128, 512), F32),
            pltpu.VMEM((256, 512), F32),
            pltpu.VMEM((128, 128), F32),
        ],
        compiler_params=pltpu.CompilerParams(vmem_limit_bytes=48 * 1024 * 1024),
        cost_estimate=pl.CostEstimate(
            flops=6_000_000_000, bytes_accessed=8_000_000, transcendentals=1_600_000
        ),
    )(at, mine, sib, ws, wt, wo, wr, edge_mine, edge_sib)


def per_device(
    node_embed, node_cotan, radial, source, target, edge_count, w_source, w_target, w_out, w_radial
):
    my_y, my_x = lax.axis_index("y"), lax.axis_index("x")
    my_z, my_c = lax.axis_index("zhi"), lax.axis_index("core")
    cotan = node_cotan[0]

    nodes = jnp.stack(gather_from(jnp.stack([node_embed[0], cotan]), "zhi"))

    live = jnp.arange(768, dtype=jnp.int32) < edge_count[0, 0]
    ids = jnp.where(live[None], jnp.stack([source[0], target[0]]) + 1, 0)
    ids = jnp.stack([ids >> 4, ids & 15]).astype(BF).reshape(24, 128)
    edges = jnp.concatenate([radial[0], ids, jnp.zeros((8, 128), BF)])
    edges = jnp.stack(gather_from(edges, "x"))
    nodes = jnp.stack(gather_from(nodes, "x"))
    edge_sib = send(edges, "core", 1)
    node_sib = send(nodes, "core", 1)

    lane = jnp.arange(128, dtype=jnp.int32)
    sel = (
        jnp.arange(256, dtype=jnp.int32)[:, None] == ((lane >> 5) * 64 + my_c * 32 + (lane & 31))[None]
    ).astype(BF)

    def columns(weight):
        part = lax.dynamic_slice_in_dim(weight, my_x * 256, 256, 1)
        return dot(part, sel).astype(BF)

    wo = lax.dynamic_slice_in_dim(w_out, my_x * 256, 256, 0).reshape(4, 2, 32, 1024)
    wo = pick(wo, my_c, 1).reshape(128, 1024)
    s_both, grads = edge_pass(
        jnp.stack([my_y, my_x, my_z, my_c]).astype(jnp.int32),
        nodes,
        node_sib,
        columns(w_source),
        columns(w_target),
        wo,
        columns(w_radial).T,
        edges,
        edge_sib,
    )

    y_parts = trade([grads[o] for o in range(4)], "y")
    s_both = total(trade([s_both[o] for o in range(4)], "zhi")).astype(BF)
    summed = total(y_parts).astype(BF)
    w_st = summed[:512].reshape(4, 4, 2, 16, 128)
    w_o = summed[512:768].reshape(4, 64, 128)
    w_r = summed[768:]

    def z_piece(o):
        at = (my_z + o) & 3
        return jnp.concatenate([pick(w_st, at, 1).reshape(128, 128), pick(w_o, at, 0), w_r])

    s_parts = trade([s_both[o] for o in range(4)], "x")
    parts = trade([z_piece(o) for o in range(4)], "zhi")
    s_both = jnp.stack(s_parts)
    s_both = trade([s_both[:, 0], s_both[:, 1]], "core")
    s_both = jnp.stack([in_order([s[o] for o in range(4)], my_x) for s in s_both])
    s_both = jnp.stack([pick(s_both, my_c, 0), pick(s_both, 1 - my_c, 0)])
    s_own = natural(s_both.transpose(2, 3, 1, 0, 4).reshape(32, 4, 2, 128), 32).reshape(2, 16, 1024)
    node_grad = (
        cotan.astype(F32)
        + dot(s_own[0], w_source, ((1,), (1,)))
        + dot(s_own[1], w_target, ((1,), (1,)))
    )
    radial_part = total([in_order([p[192:] for p in parts], my_z)[a] for a in range(4)])
    summed = jnp.concatenate([total([p[:192] for p in parts]), radial_part]).astype(BF)
    summed = total(gather_from(summed, "zlo")).astype(BF)
    w_st = summed[:128].reshape(4, 32, 128)
    w_o = summed[128:192].reshape(4, 16, 128)
    w_r = summed[192:]

    parts = trade([jnp.concatenate([pick(w_st, (my_x + o) & 3, 0), w_r]) for o in range(4)], "x")
    parts = in_order(parts, my_x)
    w_st, w_r = parts[:, :32].reshape(4, 2, 16, 128), parts[:, 32:]

    def c_piece(at):
        return jnp.concatenate([pick(w_st, at, 1), w_r], 1)

    mine, other = trade([c_piece(my_c), c_piece(1 - my_c)], "core")
    both = jnp.stack([mine, other])
    both = jnp.stack([pick(both, my_c, 0), pick(both, 1 - my_c, 0)])
    rows = natural(both.transpose(2, 1, 0, 3).reshape(48, 4, 2, 128), 48)
    w_o = w_o.transpose(1, 0, 2).reshape(8, 1024)
    rows = in_order(trade([jnp.concatenate([rows, w_o])] * 4, "y"), my_y).astype(F32)
    grad_out = rows[:, 48:].reshape(2, 2, 16, 512).transpose(1, 2, 0, 3).reshape(32, 1024)
    return (
        node_grad[None],
        rows[:2, :16].reshape(32, 1024),
        rows[2:, :16].reshape(32, 1024),
        grad_out,
        rows[:, 16:48].reshape(128, 1024),
    )


def solution(mesh):
    fine = Mesh(mesh.devices.reshape(2, 4, 4, 4, 2), ("zlo", "y", "x", "zhi", "core"))
    dp, graph = ("zlo", "y"), ("x", "zhi", "core")
    placed = (
        P(dp, graph, None),
        P(dp, graph, None),
        P(dp, graph, None),
        P(dp, graph),
        P(dp, graph),
        P(dp, graph),
        P(),
        P(),
        P(),
        P(),
    )
    return jax.shard_map(
        per_device,
        mesh=fine,
        in_specs=placed,
        out_specs=(
            P(dp, graph, None),
            P(graph, None),
            P(graph, None),
            P(graph, None),
            P(),
        ),
        check_vma=False,
    )
```

```python
import jax
import jax.numpy as jnp
from jax import lax
from jax.experimental import pallas as pl
from jax.experimental.pallas import tpu as pltpu
from jax.sharding import Mesh
from jax.sharding import PartitionSpec as P

BF = jnp.bfloat16
F32 = jnp.float32


def dot(left, right, dims=((1,), (0,))):
    return lax.dot_general(left, right, (dims, ((), ())), preferred_element_type=F32)


def pick(array, index, axis):
    return lax.dynamic_index_in_dim(array, index, axis, keepdims=False)


def send(array, axis, offset):
    size = lax.axis_size(axis)
    return lax.ppermute(array, axis, [(i, (i + offset) % size) for i in range(size)])


def gather_from(array, axis):
    return [array] + [send(array, axis, -o) for o in range(1, lax.axis_size(axis))]


def trade(pieces, axis):
    return [pieces[0]] + [send(pieces[o], axis, o) for o in range(1, len(pieces))]


def total(parts):
    out = parts[0].astype(F32)
    for part in parts[1:]:
        out = out + part.astype(F32)
    return out


def in_order(parts, me):
    size = len(parts)
    stacked = jnp.stack(parts)
    return jnp.stack([pick(stacked, (me - a) % size, 0) for a in range(size)])


def natural(array, lead):
    return array.reshape(lead, 4, 2, 4, 32).transpose(0, 1, 3, 2, 4).reshape(lead, 1024)


def edge_kernel(
    at_ref, mine_ref, sib_ref, edge_mine_ref, edge_sib_ref, ws, wt, wo, wr,
    *refs
):
    sums_refs, grad_refs = refs[:4], refs[4:8]
    grads_ref, embed, cotan, p_s, p_tq, w_r, acc_s, acc_t, acc_r = refs[8:]
    my_y, my_x, my_z, my_c = (at_ref[i] for i in range(4))

    def own(rows):
        parts = rows.reshape(4, 2, 32, rows.shape[1])
        return jnp.where(my_c == 0, parts[:, 0], parts[:, 1]).reshape(128, rows.shape[1])

    for half, ref in enumerate((mine_ref, sib_ref)):
        rows = pl.ds(half * 256, 256)
        embed[rows] = ref[:, :, 0].reshape(256, 1024)
        cotan[rows] = ref[:, :, 1].reshape(256, 1024)
    acc_s[...] = jnp.zeros_like(acc_s)
    acc_t[...] = jnp.zeros_like(acc_t)
    acc_r[...] = jnp.zeros_like(acc_r)
    p_s[...] = own(dot(embed[...], ws[...]).T).astype(BF)
    p_tq[:128] = own(dot(embed[...], wt[...]).T).astype(BF)
    p_tq[128:] = dot(own(wo[...]), cotan[...], ((1,), (1,))).astype(BF)
    w_r[...] = own(wr[...].astype(F32).T).astype(BF)
    spot = lax.broadcasted_iota(jnp.int32, (512, 768), 0).astype(jnp.int16)

    def block(ref, i):
        radial = ref[i, :768]
        coded = ref[i, 768:].astype(F32)
        node = (coded[:12] * 16.0 + coded[12:24]).astype(jnp.int32) - 1
        far_z = ((node >> 5) - my_z) & 3
        far_x = ((node >> 7) - my_x) & 3
        far_c = ((node >> 4) & 1) ^ my_c
        place = (far_c * 16 + far_x * 4 + far_z) * 16 + (node & 15)
        place = jnp.where(node >= 0, place, -1)

        def hot(first):
            row = jnp.concatenate([place[first + i : first + i + 1] for i in range(6)], axis=1)
            return jnp.where(spot == row.astype(jnp.int16), BF(1), BF(0))

        hot_s, hot_t = hot(0), hot(6)
        col = place.T
        spot_n = lax.broadcasted_iota(jnp.int32, (768, 512), 1).astype(jnp.int16)

        def hot_n(first):
            column = jnp.concatenate([col[:, first + i : first + i + 1] for i in range(6)], axis=0)
            return jnp.where(spot_n == jnp.broadcast_to(column, (768, 512)).astype(jnp.int16), BF(1), BF(0))

        both = dot(p_tq[...], hot_t)
        pre = dot(p_s[...], hot_s) + both[:128]
        gmsg = both[128:]
        rad = dot(w_r[...], radial, ((1,), (1,)))
        sig = 1.0 / (1.0 + jnp.exp(-pre))
        act = pre * sig
        message = (act * rad).astype(BF)
        grad_rad = (gmsg * act).astype(BF)
        grad_pre = (gmsg * rad * (sig + act * (1.0 - sig))).astype(BF)
        acc_t[...] += dot(jnp.concatenate([message, grad_pre]), hot_n(6))
        acc_s[...] += dot(grad_pre, hot_n(0))
        acc_r[...] += dot(grad_rad, radial)

    @pl.loop(0, 4)
    def _(i):
        block(edge_mine_ref, i)
        block(edge_sib_ref, i)

    for mat, flat in enumerate((acc_s[...], acc_t[128:])):
        nodes = flat.T.astype(BF)
        for c in range(2):
            for x in range(4):
                for z in range(4):
                    first = (c * 16 + x * 4 + z) * 16
                    sums_refs[z][x, c, mat] = nodes[first : first + 16]
        grad = dot(flat.astype(BF), embed[...]).T.astype(BF)
        for h in range(2):
            to = (2 * mat + h - my_y) & 3
            for i in range(32):
                grads_ref[to, i * 16 : i * 16 + 16] = grad[i * 32 + h * 16 : i * 32 + h * 16 + 16]
    grad = dot(acc_t[:128].astype(BF), cotan[...]).astype(BF)
    for k in range(2):
        for h in range(2):
            to = (2 * k + h - my_y) & 3
            for z in range(4):
                for b in range(4):
                    first, at = z * 32 + h * 16, 512 + (z * 4 + b) * 16
                    cols = slice(k * 512 + b * 128, k * 512 + b * 128 + 128)
                    grads_ref[to, at : at + 16] = grad[first : first + 16, cols]
    grad = acc_r[...].T.astype(BF)
    for y in range(4):
        grads_ref[(y - my_y) & 3, 768:800] = grad[y * 32 : y * 32 + 32]
    for o in range(4):
        grad_refs[o][...] = grads_ref[o]


def edge_pass(at, mine, sib, edge_mine, edge_sib, ws, wt, wo, wr):
    vmem = pl.BlockSpec(memory_space=pltpu.VMEM)
    return pl.pallas_call(
        edge_kernel,
        in_specs=[pl.BlockSpec(memory_space=pltpu.SMEM)] + [vmem] * 8,
        out_specs=[vmem] * 8,
        out_shape=[jax.ShapeDtypeStruct((4, 2, 2, 16, 128), BF)] * 4
        + [jax.ShapeDtypeStruct((800, 128), BF)] * 4,
        scratch_shapes=[
            pltpu.VMEM((4, 800, 128), BF),
            pltpu.VMEM((512, 1024), BF),
            pltpu.VMEM((512, 1024), BF),
            pltpu.VMEM((128, 512), BF),
            pltpu.VMEM((256, 512), BF),
            pltpu.VMEM((128, 128), BF),
            pltpu.VMEM((128, 512), F32),
            pltpu.VMEM((256, 512), F32),
            pltpu.VMEM((128, 128), F32),
        ],
        compiler_params=pltpu.CompilerParams(vmem_limit_bytes=16 * 1024 * 1024),
        cost_estimate=pl.CostEstimate(
            flops=6_000_000_000, bytes_accessed=8_000_000, transcendentals=1_600_000
        ),
    )(at, mine, sib, edge_mine, edge_sib, ws, wt, wo, wr)


def node_kernel(sums_ref, cotan_ref, ws_ref, wt_ref, out_ref):
    out_ref[...] = cotan_ref[...].astype(F32) + (
        dot(ws_ref[...], sums_ref[:16], ((1,), (1,))) + dot(wt_ref[...], sums_ref[16:], ((1,), (1,)))
    ).T


def node_pass(sums, cotan, ws, wt):
    vmem = pl.BlockSpec(memory_space=pltpu.VMEM)
    return pl.pallas_call(
        node_kernel,
        in_specs=[vmem] * 4,
        out_specs=vmem,
        out_shape=jax.ShapeDtypeStruct((16, 1024), F32),
        compiler_params=pltpu.CompilerParams(vmem_limit_bytes=8 * 1024 * 1024),
        cost_estimate=pl.CostEstimate(flops=70_000_000, bytes_accessed=4_300_000, transcendentals=0),
    )(sums, cotan, ws, wt)


def per_device(
    node_embed, node_cotan, radial, source, target, edge_count, w_source, w_target, w_out, w_radial
):
    my_y, my_x = lax.axis_index("y"), lax.axis_index("x")
    my_z, my_c = lax.axis_index("zhi"), lax.axis_index("core")
    cotan = node_cotan[0]

    nodes = jnp.stack(gather_from(jnp.concatenate([node_embed[0], cotan]).reshape(2, 16, 1024), "zhi"))

    live = jnp.arange(768, dtype=jnp.int32) < edge_count[0, 0]
    ids = jnp.where(live[None], jnp.stack([source[0], target[0]]) + 1, 0)
    ids = jnp.stack([ids >> 4, ids & 15]).astype(BF).reshape(24, 128)
    edges = jnp.concatenate([radial[0], ids, jnp.zeros((8, 128), BF)])
    edges = jnp.stack(gather_from(edges, "x"))
    edge_sib = send(edges, "core", 1)
    nodes = jnp.stack(gather_from(nodes, "x"))

    def mine(weight, axis):
        return lax.dynamic_slice_in_dim(weight, my_x * 256, 256, axis)

    weights = (mine(w_source, 1), mine(w_target, 1), mine(w_out, 0), mine(w_radial, 1))
    node_sib = send(nodes, "core", 1)
    at = jnp.stack([my_y, my_x, my_z, my_c]).astype(jnp.int32)
    out = edge_pass(at, nodes, node_sib, edges, edge_sib, *weights)
    sums, grads = out[:4], out[4:]

    y_parts = trade(grads, "y")
    sums = total(trade(sums, "zhi")).astype(BF).reshape(4, 64, 128)
    summed = total(y_parts).astype(BF)
    w_st = summed[:512].reshape(4, 4, 2, 16, 128)
    w_o = summed[512:768].reshape(4, 64, 128)
    w_r = summed[768:]

    def z_piece(o):
        at = (my_z + o) & 3
        return jnp.concatenate([pick(w_st, at, 1).reshape(128, 128), pick(w_o, at, 0), w_r])

    parts = trade([z_piece(o) for o in range(4)], "zhi")
    radial_part = total([in_order([p[192:] for p in parts], my_z)[a] for a in range(4)])
    summed = jnp.concatenate([total([p[:192] for p in parts]), radial_part]).astype(BF)
    summed = total(gather_from(summed, "zlo")).astype(BF)
    w_st = summed[:128].reshape(4, 32, 128)
    w_o = summed[128:192].reshape(4, 16, 128).transpose(1, 0, 2).reshape(8, 1024)
    w_r = summed[192:]

    parts = [jnp.concatenate([sums[o], pick(w_st, (my_x + o) & 3, 0), w_r]) for o in range(4)]
    parts = in_order(trade(parts, "x"), my_x)
    sums, w_st = parts[:, :64].reshape(4, 2, 32, 128), parts[:, 64:96].reshape(4, 2, 16, 128)

    def c_piece(o):
        return jnp.concatenate([sums[:, o], pick(w_st, my_c ^ o, 1), parts[:, 96:]], 1)

    both = jnp.stack(trade([c_piece(0), c_piece(1)], "core"))
    both = jnp.stack([pick(both, my_c, 0), pick(both, 1 - my_c, 0)])
    rows = natural(both.transpose(2, 1, 0, 3).reshape(80, 4, 2, 128), 80)
    node_grad = node_pass(rows[:32], cotan, w_source, w_target)
    rows = in_order(trade([jnp.concatenate([rows[32:], w_o])] * 4, "y"), my_y).astype(F32)
    grad_out = rows[:, 48:].reshape(2, 2, 16, 512).transpose(1, 2, 0, 3).reshape(32, 1024)
    return (
        node_grad[None],
        rows[:2, :16].reshape(32, 1024),
        rows[2:, :16].reshape(32, 1024),
        grad_out,
        rows[:, 16:48].reshape(128, 1024),
    )


def solution(mesh):
    fine = Mesh(mesh.devices.reshape(2, 4, 4, 4, 2), ("zlo", "y", "x", "zhi", "core"))
    dp, graph = ("zlo", "y"), ("x", "zhi", "core")
    placed = (
        P(dp, graph, None),
        P(dp, graph, None),
        P(dp, graph, None),
        P(dp, graph),
        P(dp, graph),
        P(dp, graph),
        P(),
        P(),
        P(),
        P(),
    )
    return jax.shard_map(
        per_device,
        mesh=fine,
        in_specs=placed,
        out_specs=(
            P(dp, graph, None),
            P(graph, None),
            P(graph, None),
            P(graph, None),
            P(),
        ),
        check_vma=False,
    )
```

```python
import jax
import jax.numpy as jnp
from jax import lax
from jax.experimental import pallas as pl
from jax.experimental.pallas import tpu as pltpu
from jax.sharding import Mesh
from jax.sharding import PartitionSpec as P

BF = jnp.bfloat16
F32 = jnp.float32


def dot(left, right, dims=((1,), (0,))):
    return lax.dot_general(left, right, (dims, ((), ())), preferred_element_type=F32)


def pick(array, index, axis):
    return lax.dynamic_index_in_dim(array, index, axis, keepdims=False)


def send(array, axis, offset):
    size = lax.axis_size(axis)
    return lax.ppermute(array, axis, [(i, (i + offset) % size) for i in range(size)])


def gather_from(array, axis):
    return [array] + [send(array, axis, -o) for o in range(1, lax.axis_size(axis))]


def trade(pieces, axis):
    return [pieces[0]] + [send(pieces[o], axis, o) for o in range(1, len(pieces))]


def total(parts):
    out = parts[0].astype(F32)
    for part in parts[1:]:
        out = out + part.astype(F32)
    return out


def in_order(parts, me):
    size = len(parts)
    stacked = jnp.stack(parts)
    return jnp.stack([pick(stacked, (me - a) % size, 0) for a in range(size)])


def natural(array, lead):
    return array.reshape(lead, 4, 2, 4, 32).transpose(0, 1, 3, 2, 4).reshape(lead, 1024)


def edge_kernel(
    at_ref, mine_ref, sib_ref, edge_mine_ref, edge_sib_ref, ws, wt, wo, wr,
    *refs
):
    sums_refs, grad_refs = refs[:4], refs[4:8]
    grads_ref, embed, cotan, p_s, p_tq, w_r, acc_s, acc_t, acc_r = refs[8:]
    my_y, my_x, my_z, my_c = (at_ref[i] for i in range(4))

    def own(rows):
        parts = rows.reshape(4, 2, 32, rows.shape[1])
        return jnp.where(my_c == 0, parts[:, 0], parts[:, 1]).reshape(128, rows.shape[1])

    for half, ref in enumerate((mine_ref, sib_ref)):
        rows = pl.ds(half * 256, 256)
        embed[rows] = ref[:, :, 0].reshape(256, 1024)
        cotan[rows] = ref[:, :, 1].reshape(256, 1024)
    acc_s[...] = jnp.zeros_like(acc_s)
    acc_t[...] = jnp.zeros_like(acc_t)
    acc_r[...] = jnp.zeros_like(acc_r)
    p_s[...] = own(dot(embed[...], ws[...]).T).astype(BF)
    p_tq[:128] = own(dot(embed[...], wt[...]).T).astype(BF)
    p_tq[128:] = dot(own(wo[...]), cotan[...], ((1,), (1,))).astype(BF)
    w_r[...] = own(wr[...].astype(F32).T).astype(BF)
    spot = lax.broadcasted_iota(jnp.int32, (512, 768), 0).astype(jnp.int16)

    def block(ref, i):
        radial = ref[i, :768]
        coded = ref[i, 768:].astype(F32)
        node = (coded[:12] * 16.0 + coded[12:24]).astype(jnp.int32) - 1
        far_z = ((node >> 5) - my_z) & 3
        far_x = ((node >> 7) - my_x) & 3
        far_c = ((node >> 4) & 1) ^ my_c
        place = (far_c * 16 + far_x * 4 + far_z) * 16 + (node & 15)
        place = jnp.where(node >= 0, place, -1)

        def hot(first):
            row = jnp.concatenate([place[first + i : first + i + 1] for i in range(6)], axis=1)
            return jnp.where(spot == row.astype(jnp.int16), BF(1), BF(0))

        hot_s, hot_t = hot(0), hot(6)
        col = place.T
        spot_n = lax.broadcasted_iota(jnp.int32, (768, 512), 1).astype(jnp.int16)

        def hot_n(first):
            column = jnp.concatenate([col[:, first + i : first + i + 1] for i in range(6)], axis=0)
            return jnp.where(spot_n == jnp.broadcast_to(column, (768, 512)).astype(jnp.int16), BF(1), BF(0))

        both = dot(p_tq[...], hot_t)
        pre = dot(p_s[...], hot_s) + both[:128]
        gmsg = both[128:]
        rad = dot(w_r[...], radial, ((1,), (1,)))
        sig = 1.0 / (1.0 + jnp.exp(-pre))
        act = pre * sig
        message = (act * rad).astype(BF)
        grad_rad = (gmsg * act).astype(BF)
        grad_pre = (gmsg * rad * (sig + act * (1.0 - sig))).astype(BF)
        acc_t[...] += dot(jnp.concatenate([message, grad_pre]), hot_n(6))
        acc_s[...] += dot(grad_pre, hot_n(0))
        acc_r[...] += dot(grad_rad, radial)

    for i in range(4):
        block(edge_mine_ref, i)
        block(edge_sib_ref, i)

    for mat, flat in enumerate((acc_s[...], acc_t[128:])):
        nodes = flat.T.astype(BF)
        for c in range(2):
            for x in range(4):
                for z in range(4):
                    first = (c * 16 + x * 4 + z) * 16
                    sums_refs[z][x, c, mat] = nodes[first : first + 16]
        grad = dot(flat.astype(BF), embed[...]).T.astype(BF)
        for h in range(2):
            to = (2 * mat + h - my_y) & 3
            for i in range(32):
                grads_ref[to, i * 16 : i * 16 + 16] = grad[i * 32 + h * 16 : i * 32 + h * 16 + 16]
    grad = dot(acc_t[:128].astype(BF), cotan[...]).astype(BF)
    for k in range(2):
        for h in range(2):
            to = (2 * k + h - my_y) & 3
            for z in range(4):
                for b in range(4):
                    first, at = z * 32 + h * 16, 512 + (z * 4 + b) * 16
                    cols = slice(k * 512 + b * 128, k * 512 + b * 128 + 128)
                    grads_ref[to, at : at + 16] = grad[first : first + 16, cols]
    grad = acc_r[...].T.astype(BF)
    for y in range(4):
        grads_ref[(y - my_y) & 3, 768:800] = grad[y * 32 : y * 32 + 32]
    for o in range(4):
        grad_refs[o][...] = grads_ref[o]


def edge_pass(at, mine, sib, edge_mine, edge_sib, ws, wt, wo, wr):
    vmem = pl.BlockSpec(memory_space=pltpu.VMEM)
    return pl.pallas_call(
        edge_kernel,
        in_specs=[pl.BlockSpec(memory_space=pltpu.SMEM)] + [vmem] * 8,
        out_specs=[vmem] * 8,
        out_shape=[jax.ShapeDtypeStruct((4, 2, 2, 16, 128), BF)] * 4
        + [jax.ShapeDtypeStruct((800, 128), BF)] * 4,
        scratch_shapes=[
            pltpu.VMEM((4, 800, 128), BF),
            pltpu.VMEM((512, 1024), BF),
            pltpu.VMEM((512, 1024), BF),
            pltpu.VMEM((128, 512), BF),
            pltpu.VMEM((256, 512), BF),
            pltpu.VMEM((128, 128), BF),
            pltpu.VMEM((128, 512), F32),
            pltpu.VMEM((256, 512), F32),
            pltpu.VMEM((128, 128), F32),
        ],
        compiler_params=pltpu.CompilerParams(vmem_limit_bytes=16 * 1024 * 1024),
        cost_estimate=pl.CostEstimate(
            flops=6_000_000_000, bytes_accessed=8_000_000, transcendentals=1_600_000
        ),
    )(at, mine, sib, edge_mine, edge_sib, ws, wt, wo, wr)


def node_kernel(sums_ref, cotan_ref, ws_ref, wt_ref, out_ref):
    out_ref[...] = cotan_ref[...].astype(F32) + (
        dot(ws_ref[...], sums_ref[:16], ((1,), (1,))) + dot(wt_ref[...], sums_ref[16:], ((1,), (1,)))
    ).T


def node_pass(sums, cotan, ws, wt):
    vmem = pl.BlockSpec(memory_space=pltpu.VMEM)
    return pl.pallas_call(
        node_kernel,
        in_specs=[vmem] * 4,
        out_specs=vmem,
        out_shape=jax.ShapeDtypeStruct((16, 1024), F32),
        compiler_params=pltpu.CompilerParams(vmem_limit_bytes=8 * 1024 * 1024),
        cost_estimate=pl.CostEstimate(flops=70_000_000, bytes_accessed=4_300_000, transcendentals=0),
    )(sums, cotan, ws, wt)


def per_device(
    node_embed, node_cotan, radial, source, target, edge_count, w_source, w_target, w_out, w_radial
):
    my_y, my_x = lax.axis_index("y"), lax.axis_index("x")
    my_z, my_c = lax.axis_index("zhi"), lax.axis_index("core")
    cotan = node_cotan[0]

    nodes = gather_from(jnp.concatenate([node_embed[0], cotan]).reshape(2, 16, 1024), "zhi")

    live = jnp.arange(768, dtype=jnp.int32) < edge_count[0, 0]
    ids = jnp.where(live[None], jnp.stack([source[0], target[0]]) + 1, 0)
    ids = jnp.stack([ids >> 4, ids & 15]).astype(BF).reshape(24, 128)
    edges = jnp.concatenate([radial[0], ids, jnp.zeros((8, 128), BF)])
    edges = gather_from(edges, "x")
    nodes, edges[2] = lax.optimization_barrier((nodes, edges[2]))
    edges = jnp.stack(edges)
    edge_sib = send(edges, "core", 1)
    nodes = jnp.stack(gather_from(jnp.stack(nodes), "x"))

    def mine(weight, axis):
        return lax.dynamic_slice_in_dim(weight, my_x * 256, 256, axis)

    weights = (mine(w_source, 1), mine(w_target, 1), mine(w_out, 0), mine(w_radial, 1))
    node_sib = send(nodes, "core", 1)
    at = jnp.stack([my_y, my_x, my_z, my_c]).astype(jnp.int32)
    out = edge_pass(at, nodes, node_sib, edges, edge_sib, *weights)
    sums, grads = out[:4], out[4:]

    y_parts = trade(grads, "y")
    sums = trade(sums, "zhi")
    summed = total(y_parts).astype(BF)
    w_st = summed[:512].reshape(4, 4, 2, 16, 128)
    w_o = summed[512:768].reshape(4, 64, 128)
    w_r = summed[768:]

    def z_piece(o):
        at = (my_z + o) & 3
        return jnp.concatenate([pick(w_st, at, 1).reshape(128, 128), pick(w_o, at, 0), w_r])

    parts = trade([z_piece(o) for o in range(4)], "zhi")
    parts, sums = lax.optimization_barrier((parts, sums))
    sums = total(sums).astype(BF).reshape(4, 64, 128)
    radial_part = total([in_order([p[192:] for p in parts], my_z)[a] for a in range(4)])
    summed = jnp.concatenate([total([p[:192] for p in parts]), radial_part]).astype(BF)
    summed = total(gather_from(summed, "zlo")).astype(BF)
    w_st = summed[:128].reshape(4, 32, 128)
    w_o = summed[128:192].reshape(4, 16, 128).transpose(1, 0, 2).reshape(8, 1024)
    w_r = summed[192:]

    parts = [jnp.concatenate([sums[o], pick(w_st, (my_x + o) & 3, 0), w_r]) for o in range(4)]
    parts = in_order(trade(parts, "x"), my_x)
    sums, w_st = parts[:, :64].reshape(4, 2, 32, 128), parts[:, 64:96].reshape(4, 2, 16, 128)

    def c_piece(o):
        return jnp.concatenate([sums[:, o], pick(w_st, my_c ^ o, 1), parts[:, 96:]], 1)

    both = jnp.stack(trade([c_piece(0), c_piece(1)], "core"))
    both = jnp.stack([pick(both, my_c, 0), pick(both, 1 - my_c, 0)])
    rows = natural(both.transpose(2, 1, 0, 3).reshape(80, 4, 2, 128), 80)
    node_grad = node_pass(rows[:32], cotan, w_source, w_target)
    rows = in_order(trade([jnp.concatenate([rows[32:], w_o])] * 4, "y"), my_y).astype(F32)
    grad_out = rows[:, 48:].reshape(2, 2, 16, 512).transpose(1, 2, 0, 3).reshape(32, 1024)
    return (
        node_grad[None],
        rows[:2, :16].reshape(32, 1024),
        rows[2:, :16].reshape(32, 1024),
        grad_out,
        rows[:, 16:48].reshape(128, 1024),
    )


def solution(mesh):
    fine = Mesh(mesh.devices.reshape(2, 4, 4, 4, 2), ("zlo", "y", "x", "zhi", "core"))
    dp, graph = ("zlo", "y"), ("x", "zhi", "core")
    placed = (
        P(dp, graph, None),
        P(dp, graph, None),
        P(dp, graph, None),
        P(dp, graph),
        P(dp, graph),
        P(dp, graph),
        P(),
        P(),
        P(),
        P(),
    )
    return jax.shard_map(
        per_device,
        mesh=fine,
        in_specs=placed,
        out_specs=(
            P(dp, graph, None),
            P(graph, None),
            P(graph, None),
            P(graph, None),
            P(),
        ),
        check_vma=False,
    )
```

```python
import jax
import jax.numpy as jnp
from jax import lax
from jax.experimental import pallas as pl
from jax.experimental.pallas import tpu as pltpu
from jax.sharding import Mesh
from jax.sharding import PartitionSpec as P

BF = jnp.bfloat16
F32 = jnp.float32


def dot(left, right, dims=((1,), (0,))):
    return lax.dot_general(left, right, (dims, ((), ())), preferred_element_type=F32)


def pick(array, index, axis):
    return lax.dynamic_index_in_dim(array, index, axis, keepdims=False)


def send(array, axis, offset):
    size = lax.axis_size(axis)
    return lax.ppermute(array, axis, [(i, (i + offset) % size) for i in range(size)])


def gather_from(array, axis):
    return [array] + [send(array, axis, -o) for o in range(1, lax.axis_size(axis))]


def trade(pieces, axis):
    return [pieces[0]] + [send(pieces[o], axis, o) for o in range(1, len(pieces))]


def total(parts):
    out = parts[0].astype(F32)
    for part in parts[1:]:
        out = out + part.astype(F32)
    return out


def in_order(parts, me):
    size = len(parts)
    stacked = jnp.stack(parts)
    return jnp.stack([pick(stacked, (me - a) % size, 0) for a in range(size)])


def natural(array, lead):
    return array.reshape(lead, 4, 2, 4, 32).transpose(0, 1, 3, 2, 4).reshape(lead, 1024)


def edge_blocks(at_ref, refs, p_s, p_tq, w_r, acc_s, acc_t, acc_r):
    my_y, my_x, my_z, my_c = (at_ref[i] for i in range(4))
    spot = lax.broadcasted_iota(jnp.int32, (512, 768), 0).astype(jnp.int16)

    for i in range(4):
        edges = refs[i % 2][i // 2]
        radial = edges[:768]
        coded = edges[768:].astype(F32)
        node = (coded[:12] * 16.0 + coded[12:24]).astype(jnp.int32) - 1
        far_z = ((node >> 5) - my_z) & 3
        far_x = ((node >> 7) - my_x) & 3
        far_c = ((node >> 4) & 1) ^ my_c
        place = (far_c * 16 + far_x * 4 + far_z) * 16 + (node & 15)
        place = jnp.where(node >= 0, place, -1)

        def hot(first):
            row = jnp.concatenate([place[first + i : first + i + 1] for i in range(6)], axis=1)
            return jnp.where(spot == row.astype(jnp.int16), BF(1), BF(0))

        hot_s, hot_t = hot(0), hot(6)
        col = place.T
        spot_n = lax.broadcasted_iota(jnp.int32, (768, 512), 1).astype(jnp.int16)

        def hot_n(first):
            column = jnp.concatenate([col[:, first + i : first + i + 1] for i in range(6)], axis=0)
            return jnp.where(spot_n == jnp.broadcast_to(column, (768, 512)).astype(jnp.int16), BF(1), BF(0))

        both = dot(p_tq[...], hot_t)
        pre = dot(p_s[...], hot_s) + both[:128]
        gmsg = both[128:]
        rad = dot(w_r[...], radial, ((1,), (1,)))
        sig = 1.0 / (1.0 + jnp.exp(-pre))
        act = pre * sig
        message = (act * rad).astype(BF)
        grad_rad = (gmsg * act).astype(BF)
        grad_pre = (gmsg * rad * (sig + act * (1.0 - sig))).astype(BF)
        acc_t[...] += dot(jnp.concatenate([message, grad_pre]), hot_n(6))
        acc_s[...] += dot(grad_pre, hot_n(0))
        acc_r[...] += dot(grad_rad, radial)


def first_kernel(
    at_ref, mine_ref, sib_ref, edge_ref, edge_sib_ref, ws, wt, wo, wr,
    embed, cotan, p_s, p_tq, w_r, acc_s, acc_t, acc_r
):
    my_c = at_ref[3]

    def own(rows):
        parts = rows.reshape(4, 2, 32, rows.shape[1])
        return jnp.where(my_c == 0, parts[:, 0], parts[:, 1]).reshape(128, rows.shape[1])

    for half, ref in enumerate((mine_ref, sib_ref)):
        rows = pl.ds(half * 256, 256)
        embed[rows] = ref[:, :, 0].reshape(256, 1024)
        cotan[rows] = ref[:, :, 1].reshape(256, 1024)
    acc_s[...] = jnp.zeros_like(acc_s)
    acc_t[...] = jnp.zeros_like(acc_t)
    acc_r[...] = jnp.zeros_like(acc_r)
    p_s[...] = own(dot(embed[...], ws[...]).T).astype(BF)
    p_tq[:128] = own(dot(embed[...], wt[...]).T).astype(BF)
    p_tq[128:] = dot(own(wo[...]), cotan[...], ((1,), (1,))).astype(BF)
    w_r[...] = own(wr[...].astype(F32).T).astype(BF)
    edge_blocks(at_ref, (edge_ref, edge_sib_ref), p_s, p_tq, w_r, acc_s, acc_t, acc_r)


def second_kernel(
    at_ref, edge_ref, edge_sib_ref, embed, cotan, p_s, p_tq, w_r, in_s, in_t, in_r, *refs
):
    sums_refs, grad_refs = refs[:4], refs[4:8]
    grads_ref, acc_s, acc_t, acc_r = refs[8:]
    my_y, my_x, my_z, my_c = (at_ref[i] for i in range(4))
    acc_s[...] = in_s[...]
    acc_t[...] = in_t[...]
    acc_r[...] = in_r[...]
    edge_blocks(at_ref, (edge_ref, edge_sib_ref), p_s, p_tq, w_r, acc_s, acc_t, acc_r)

    for mat, flat in enumerate((acc_s[...], acc_t[128:])):
        nodes = flat.T.astype(BF)
        for c in range(2):
            for x in range(4):
                for z in range(4):
                    first = (c * 16 + x * 4 + z) * 16
                    sums_refs[z][x, c, mat] = nodes[first : first + 16]
        grad = dot(flat.astype(BF), embed[...]).T.astype(BF)
        for h in range(2):
            to = (2 * mat + h - my_y) & 3
            for i in range(32):
                grads_ref[to, i * 16 : i * 16 + 16] = grad[i * 32 + h * 16 : i * 32 + h * 16 + 16]
    grad = dot(acc_t[:128].astype(BF), cotan[...]).astype(BF)
    for k in range(2):
        for h in range(2):
            to = (2 * k + h - my_y) & 3
            for z in range(4):
                for b in range(4):
                    first, at = z * 32 + h * 16, 512 + (z * 4 + b) * 16
                    cols = slice(k * 512 + b * 128, k * 512 + b * 128 + 128)
                    grads_ref[to, at : at + 16] = grad[first : first + 16, cols]
    grad = acc_r[...].T.astype(BF)
    for y in range(4):
        grads_ref[(y - my_y) & 3, 768:800] = grad[y * 32 : y * 32 + 32]
    for o in range(4):
        grad_refs[o][...] = grads_ref[o]


def edge_pass(at, mine, sib, early, early_sib, late, late_sib, ws, wt, wo, wr):
    smem = pl.BlockSpec(memory_space=pltpu.SMEM)
    vmem = pl.BlockSpec(memory_space=pltpu.VMEM)
    half = pl.CostEstimate(
        flops=3_000_000_000, bytes_accessed=4_000_000, transcendentals=800_000
    )
    accumulators = [
        jax.ShapeDtypeStruct((128, 512), F32),
        jax.ShapeDtypeStruct((256, 512), F32),
        jax.ShapeDtypeStruct((128, 128), F32),
    ]
    state = pl.pallas_call(
        first_kernel,
        in_specs=[smem] + [vmem] * 8,
        out_specs=[vmem] * 8,
        out_shape=[
            jax.ShapeDtypeStruct((512, 1024), BF),
            jax.ShapeDtypeStruct((512, 1024), BF),
            jax.ShapeDtypeStruct((128, 512), BF),
            jax.ShapeDtypeStruct((256, 512), BF),
            jax.ShapeDtypeStruct((128, 128), BF),
        ]
        + accumulators,
        compiler_params=pltpu.CompilerParams(vmem_limit_bytes=16 * 1024 * 1024),
        cost_estimate=half,
    )(at, mine, sib, early, early_sib, ws, wt, wo, wr)
    return pl.pallas_call(
        second_kernel,
        in_specs=[smem] + [vmem] * 10,
        out_specs=[vmem] * 8,
        out_shape=[jax.ShapeDtypeStruct((4, 2, 2, 16, 128), BF)] * 4
        + [jax.ShapeDtypeStruct((800, 128), BF)] * 4,
        scratch_shapes=[pltpu.VMEM((4, 800, 128), BF)]
        + [pltpu.VMEM(leaf.shape, leaf.dtype) for leaf in accumulators],
        compiler_params=pltpu.CompilerParams(vmem_limit_bytes=16 * 1024 * 1024),
        cost_estimate=half,
    )(at, late, late_sib, *state)


def node_kernel(sums_ref, cotan_ref, ws_ref, wt_ref, out_ref):
    out_ref[...] = cotan_ref[...].astype(F32) + (
        dot(ws_ref[...], sums_ref[:16], ((1,), (1,))) + dot(wt_ref[...], sums_ref[16:], ((1,), (1,)))
    ).T


def node_pass(sums, cotan, ws, wt):
    vmem = pl.BlockSpec(memory_space=pltpu.VMEM)
    return pl.pallas_call(
        node_kernel,
        in_specs=[vmem] * 4,
        out_specs=vmem,
        out_shape=jax.ShapeDtypeStruct((16, 1024), F32),
        compiler_params=pltpu.CompilerParams(vmem_limit_bytes=8 * 1024 * 1024),
        cost_estimate=pl.CostEstimate(flops=70_000_000, bytes_accessed=4_300_000, transcendentals=0),
    )(sums, cotan, ws, wt)


def per_device(
    node_embed, node_cotan, radial, source, target, edge_count, w_source, w_target, w_out, w_radial
):
    my_y, my_x = lax.axis_index("y"), lax.axis_index("x")
    my_z, my_c = lax.axis_index("zhi"), lax.axis_index("core")
    cotan = node_cotan[0]

    nodes = gather_from(jnp.concatenate([node_embed[0], cotan]).reshape(2, 16, 1024), "zhi")

    live = jnp.arange(768, dtype=jnp.int32) < edge_count[0, 0]
    ids = jnp.where(live[None], jnp.stack([source[0], target[0]]) + 1, 0)
    ids = jnp.stack([ids >> 4, ids & 15]).astype(BF).reshape(24, 128)
    edges = jnp.concatenate([radial[0], ids, jnp.zeros((8, 128), BF)])
    edges = gather_from(edges, "x")
    nodes, edges[2] = lax.optimization_barrier((nodes, edges[2]))
    early, late = jnp.stack([edges[0], edges[2]]), jnp.stack([edges[1], edges[3]])
    early_sib = send(early, "core", 1)
    nodes = jnp.stack(gather_from(jnp.stack(nodes), "x"))

    def mine(weight, axis):
        return lax.dynamic_slice_in_dim(weight, my_x * 256, 256, axis)

    weights = (mine(w_source, 1), mine(w_target, 1), mine(w_out, 0), mine(w_radial, 1))
    nodes, late, early_sib = lax.optimization_barrier((nodes, late, early_sib))
    node_sib = send(nodes, "core", 1)
    late_sib = send(late, "core", 1)
    at = jnp.stack([my_y, my_x, my_z, my_c]).astype(jnp.int32)
    out = edge_pass(at, nodes, node_sib, early, early_sib, late, late_sib, *weights)
    sums, grads = out[:4], out[4:]

    y_parts = trade(grads, "y")
    sums = trade(sums, "zhi")
    summed = total(y_parts).astype(BF)
    w_st = summed[:512].reshape(4, 4, 2, 16, 128)
    w_o = summed[512:768].reshape(4, 64, 128)
    w_r = summed[768:]

    def z_piece(o):
        at = (my_z + o) & 3
        return jnp.concatenate([pick(w_st, at, 1).reshape(128, 128), pick(w_o, at, 0), w_r])

    parts = trade([z_piece(o) for o in range(4)], "zhi")
    parts, sums = lax.optimization_barrier((parts, sums))
    sums = total(sums).astype(BF).reshape(4, 64, 128)
    radial_part = total([in_order([p[192:] for p in parts], my_z)[a] for a in range(4)])
    summed = jnp.concatenate([total([p[:192] for p in parts]), radial_part]).astype(BF)
    summed = total(gather_from(summed, "zlo")).astype(BF)
    w_st = summed[:128].reshape(4, 32, 128)
    w_o = summed[128:192].reshape(4, 16, 128).transpose(1, 0, 2).reshape(8, 1024)
    w_r = summed[192:]

    parts = [jnp.concatenate([sums[o], pick(w_st, (my_x + o) & 3, 0), w_r]) for o in range(4)]
    parts = in_order(trade(parts, "x"), my_x)
    sums, w_st = parts[:, :64].reshape(4, 2, 32, 128), parts[:, 64:96].reshape(4, 2, 16, 128)

    def c_piece(o):
        return jnp.concatenate([sums[:, o], pick(w_st, my_c ^ o, 1), parts[:, 96:]], 1)

    both = jnp.stack(trade([c_piece(0), c_piece(1)], "core"))
    both = jnp.stack([pick(both, my_c, 0), pick(both, 1 - my_c, 0)])
    rows = natural(both.transpose(2, 1, 0, 3).reshape(80, 4, 2, 128), 80)
    node_grad = node_pass(rows[:32], cotan, w_source, w_target)
    rows = in_order(trade([jnp.concatenate([rows[32:], w_o])] * 4, "y"), my_y).astype(F32)
    grad_out = rows[:, 48:].reshape(2, 2, 16, 512).transpose(1, 2, 0, 3).reshape(32, 1024)
    return (
        node_grad[None],
        rows[:2, :16].reshape(32, 1024),
        rows[2:, :16].reshape(32, 1024),
        grad_out,
        rows[:, 16:48].reshape(128, 1024),
    )


def solution(mesh):
    fine = Mesh(mesh.devices.reshape(2, 4, 4, 4, 2), ("zlo", "y", "x", "zhi", "core"))
    dp, graph = ("zlo", "y"), ("x", "zhi", "core")
    placed = (
        P(dp, graph, None),
        P(dp, graph, None),
        P(dp, graph, None),
        P(dp, graph),
        P(dp, graph),
        P(dp, graph),
        P(),
        P(),
        P(),
        P(),
    )
    return jax.shard_map(
        per_device,
        mesh=fine,
        in_specs=placed,
        out_specs=(
            P(dp, graph, None),
            P(graph, None),
            P(graph, None),
            P(graph, None),
            P(),
        ),
        check_vma=False,
    )
```

```python
import jax
import jax.numpy as jnp
from jax import lax
from jax.experimental import pallas as pl
from jax.experimental.pallas import tpu as pltpu
from jax.sharding import Mesh
from jax.sharding import PartitionSpec as P

BF = jnp.bfloat16
F32 = jnp.float32


def dot(left, right, dims=((1,), (0,))):
    return lax.dot_general(left, right, (dims, ((), ())), preferred_element_type=F32)


def pick(array, index, axis):
    return lax.dynamic_index_in_dim(array, index, axis, keepdims=False)


def send(array, axis, offset):
    size = lax.axis_size(axis)
    return lax.ppermute(array, axis, [(i, (i + offset) % size) for i in range(size)])


def gather_from(array, axis):
    return [array] + [send(array, axis, -o) for o in range(1, lax.axis_size(axis))]


def trade(pieces, axis):
    return [pieces[0]] + [send(pieces[o], axis, o) for o in range(1, len(pieces))]


def total(parts):
    out = parts[0].astype(F32)
    for part in parts[1:]:
        out = out + part.astype(F32)
    return out


def in_order(parts, me):
    size = len(parts)
    stacked = jnp.stack(parts)
    return jnp.stack([pick(stacked, (me - a) % size, 0) for a in range(size)])


def natural(array, lead):
    return array.reshape(lead, 4, 2, 4, 32).transpose(0, 1, 3, 2, 4).reshape(lead, 1024)


def edge_blocks(at_ref, refs, p_s, p_tq, w_r, acc_s, acc_t, acc_r):
    my_y, my_x, my_z, my_c = (at_ref[i] for i in range(4))
    spot = lax.broadcasted_iota(jnp.int32, (512, 768), 0).astype(jnp.int16)

    for i in range(4):
        edges = refs[i % 2][i // 2]
        radial = edges[:768]
        coded = edges[768:].astype(F32)
        node = (coded[:12] * 16.0 + coded[12:24]).astype(jnp.int32) - 1
        far_z = ((node >> 5) - my_z) & 3
        far_x = ((node >> 7) - my_x) & 3
        far_c = ((node >> 4) & 1) ^ my_c
        place = (far_c * 16 + far_x * 4 + far_z) * 16 + (node & 15)
        place = jnp.where(node >= 0, place, -1)

        def hot(first):
            row = jnp.concatenate([place[first + i : first + i + 1] for i in range(6)], axis=1)
            return jnp.where(spot == row.astype(jnp.int16), BF(1), BF(0))

        hot_s, hot_t = hot(0), hot(6)
        col = place.T
        spot_n = lax.broadcasted_iota(jnp.int32, (768, 512), 1).astype(jnp.int16)

        def hot_n(first):
            column = jnp.concatenate([col[:, first + i : first + i + 1] for i in range(6)], axis=0)
            return jnp.where(spot_n == jnp.broadcast_to(column, (768, 512)).astype(jnp.int16), BF(1), BF(0))

        both = dot(p_tq[...], hot_t)
        pre = dot(p_s[...], hot_s) + both[:128]
        gmsg = both[128:]
        rad = dot(w_r[...], radial, ((1,), (1,)))
        sig = 1.0 / (1.0 + jnp.exp(-pre))
        act = pre * sig
        message = (act * rad).astype(BF)
        grad_rad = (gmsg * act).astype(BF)
        grad_pre = (gmsg * rad * (sig + act * (1.0 - sig))).astype(BF)
        acc_t[...] += dot(jnp.concatenate([message, grad_pre]), hot_n(6))
        acc_s[...] += dot(grad_pre, hot_n(0))
        acc_r[...] += dot(grad_rad, radial)


def first_kernel(
    at_ref, mine_ref, sib_ref, edge_ref, edge_sib_ref, ws, wt, wo, wr,
    embed, cotan, p_s, p_tq, w_r, acc_s, acc_t, acc_r
):
    my_c = at_ref[3]

    def own(rows):
        parts = rows.reshape(4, 2, 32, rows.shape[1])
        return jnp.where(my_c == 0, parts[:, 0], parts[:, 1]).reshape(128, rows.shape[1])

    for half, ref in enumerate((mine_ref, sib_ref)):
        rows = pl.ds(half * 256, 256)
        embed[rows] = ref[:, :, 0].reshape(256, 1024)
        cotan[rows] = ref[:, :, 1].reshape(256, 1024)
    acc_s[...] = jnp.zeros_like(acc_s)
    acc_t[...] = jnp.zeros_like(acc_t)
    acc_r[...] = jnp.zeros_like(acc_r)
    p_s[...] = own(dot(embed[...], ws[...]).T).astype(BF)
    p_tq[:128] = own(dot(embed[...], wt[...]).T).astype(BF)
    p_tq[128:] = dot(own(wo[...]), cotan[...], ((1,), (1,))).astype(BF)
    w_r[...] = own(wr[...].astype(F32).T).astype(BF)
    edge_blocks(at_ref, (edge_ref, edge_sib_ref), p_s, p_tq, w_r, acc_s, acc_t, acc_r)


def second_kernel(
    at_ref, edge_ref, edge_sib_ref, embed, cotan, p_s, p_tq, w_r, in_s, in_t, in_r, *refs
):
    sums_refs, grad_refs = refs[:4], refs[4:8]
    grads_ref, acc_s, acc_t, acc_r = refs[8:]
    my_y, my_x, my_z, my_c = (at_ref[i] for i in range(4))
    acc_s[...] = in_s[...]
    acc_t[...] = in_t[...]
    acc_r[...] = in_r[...]
    edge_blocks(at_ref, (edge_ref, edge_sib_ref), p_s, p_tq, w_r, acc_s, acc_t, acc_r)

    for mat, flat in enumerate((acc_s[...], acc_t[128:])):
        nodes = flat.T.astype(BF)
        for c in range(2):
            for x in range(4):
                for z in range(4):
                    first = (c * 16 + x * 4 + z) * 16
                    sums_refs[z][x, c, mat] = nodes[first : first + 16]
        grad = dot(flat.astype(BF), embed[...]).T.astype(BF)
        for h in range(2):
            to = (2 * mat + h - my_y) & 3
            for i in range(32):
                grads_ref[to, i * 16 : i * 16 + 16] = grad[i * 32 + h * 16 : i * 32 + h * 16 + 16]
    grad = dot(acc_t[:128].astype(BF), cotan[...]).astype(BF)
    for k in range(2):
        for h in range(2):
            to = (2 * k + h - my_y) & 3
            for z in range(4):
                for b in range(4):
                    first, at = z * 32 + h * 16, 512 + (z * 4 + b) * 16
                    cols = slice(k * 512 + b * 128, k * 512 + b * 128 + 128)
                    grads_ref[to, at : at + 16] = grad[first : first + 16, cols]
    grad = acc_r[...].T.astype(BF)
    for y in range(4):
        grads_ref[(y - my_y) & 3, 768:800] = grad[y * 32 : y * 32 + 32]
    for o in range(4):
        grad_refs[o][...] = grads_ref[o]


def edge_pass(at, mine, sib, early, early_sib, late, late_sib, ws, wt, wo, wr):
    smem = pl.BlockSpec(memory_space=pltpu.SMEM)
    vmem = pl.BlockSpec(memory_space=pltpu.VMEM)
    half = pl.CostEstimate(
        flops=3_000_000_000, bytes_accessed=4_000_000, transcendentals=800_000
    )
    accumulators = [
        jax.ShapeDtypeStruct((128, 512), F32),
        jax.ShapeDtypeStruct((256, 512), F32),
        jax.ShapeDtypeStruct((128, 128), F32),
    ]
    state = pl.pallas_call(
        first_kernel,
        in_specs=[smem] + [vmem] * 8,
        out_specs=[vmem] * 8,
        out_shape=[
            jax.ShapeDtypeStruct((512, 1024), BF),
            jax.ShapeDtypeStruct((512, 1024), BF),
            jax.ShapeDtypeStruct((128, 512), BF),
            jax.ShapeDtypeStruct((256, 512), BF),
            jax.ShapeDtypeStruct((128, 128), BF),
        ]
        + accumulators,
        compiler_params=pltpu.CompilerParams(vmem_limit_bytes=16 * 1024 * 1024),
        cost_estimate=half,
    )(at, mine, sib, early, early_sib, ws, wt, wo, wr)
    return pl.pallas_call(
        second_kernel,
        in_specs=[smem] + [vmem] * 10,
        out_specs=[vmem] * 8,
        out_shape=[jax.ShapeDtypeStruct((4, 2, 2, 16, 128), BF)] * 4
        + [jax.ShapeDtypeStruct((800, 128), BF)] * 4,
        scratch_shapes=[pltpu.VMEM((4, 800, 128), BF)]
        + [pltpu.VMEM(leaf.shape, leaf.dtype) for leaf in accumulators],
        compiler_params=pltpu.CompilerParams(vmem_limit_bytes=16 * 1024 * 1024),
        cost_estimate=half,
    )(at, late, late_sib, *state)


def node_kernel(sums_ref, cotan_ref, ws_ref, wt_ref, out_ref):
    out_ref[...] = cotan_ref[...].astype(F32) + (
        dot(ws_ref[...], sums_ref[:16], ((1,), (1,))) + dot(wt_ref[...], sums_ref[16:], ((1,), (1,)))
    ).T


def node_pass(sums, cotan, ws, wt):
    vmem = pl.BlockSpec(memory_space=pltpu.VMEM)
    return pl.pallas_call(
        node_kernel,
        in_specs=[vmem] * 4,
        out_specs=vmem,
        out_shape=jax.ShapeDtypeStruct((16, 1024), F32),
        compiler_params=pltpu.CompilerParams(vmem_limit_bytes=8 * 1024 * 1024),
        cost_estimate=pl.CostEstimate(flops=70_000_000, bytes_accessed=4_300_000, transcendentals=0),
    )(sums, cotan, ws, wt)


def per_device(
    node_embed, node_cotan, radial, source, target, edge_count, w_source, w_target, w_out, w_radial
):
    my_y, my_x = lax.axis_index("y"), lax.axis_index("x")
    my_z, my_c = lax.axis_index("zhi"), lax.axis_index("core")
    cotan = node_cotan[0]

    nodes = gather_from(jnp.concatenate([node_embed[0], cotan]).reshape(2, 16, 1024), "zhi")

    live = jnp.arange(768, dtype=jnp.int32) < edge_count[0, 0]
    ids = jnp.where(live[None], jnp.stack([source[0], target[0]]) + 1, 0)
    ids = jnp.stack([ids >> 4, ids & 15]).astype(BF).reshape(24, 128)
    edges = jnp.concatenate([radial[0], ids, jnp.zeros((8, 128), BF)])
    edges = gather_from(edges, "x")
    early, late = jnp.stack([edges[0], edges[2]]), jnp.stack([edges[1], edges[3]])
    early_sib = send(early, "core", 1)
    nodes = jnp.stack(gather_from(jnp.stack(nodes), "x"))

    def mine(weight, axis):
        return lax.dynamic_slice_in_dim(weight, my_x * 256, 256, axis)

    weights = (mine(w_source, 1), mine(w_target, 1), mine(w_out, 0), mine(w_radial, 1))
    nodes, late, early_sib = lax.optimization_barrier((nodes, late, early_sib))
    node_sib = send(nodes, "core", 1)
    late_sib = send(late, "core", 1)
    at = jnp.stack([my_y, my_x, my_z, my_c]).astype(jnp.int32)
    out = edge_pass(at, nodes, node_sib, early, early_sib, late, late_sib, *weights)
    sums, grads = out[:4], out[4:]

    y_parts = trade(grads, "y")
    sums = trade(sums, "zhi")
    summed = total(y_parts).astype(BF)
    w_st = summed[:512].reshape(4, 4, 2, 16, 128)
    w_o = summed[512:768].reshape(4, 64, 128)
    w_r = summed[768:]

    def z_piece(o):
        at = (my_z + o) & 3
        return jnp.concatenate([pick(w_st, at, 1).reshape(128, 128), pick(w_o, at, 0), w_r])

    parts = trade([z_piece(o) for o in range(4)], "zhi")
    parts, sums = lax.optimization_barrier((parts, sums))
    sums = total(sums).astype(BF).reshape(4, 64, 128)
    radial_part = total([in_order([p[192:] for p in parts], my_z)[a] for a in range(4)])
    summed = jnp.concatenate([total([p[:192] for p in parts]), radial_part]).astype(BF)
    summed = total(gather_from(summed, "zlo")).astype(BF)
    w_st = summed[:128].reshape(4, 32, 128)
    w_o = summed[128:192].reshape(4, 16, 128).transpose(1, 0, 2).reshape(8, 1024)
    w_r = summed[192:]

    parts = [jnp.concatenate([sums[o], pick(w_st, (my_x + o) & 3, 0), w_r]) for o in range(4)]
    parts = in_order(trade(parts, "x"), my_x)
    sums, w_st = parts[:, :64].reshape(4, 2, 32, 128), parts[:, 64:96].reshape(4, 2, 16, 128)

    def c_piece(o):
        return jnp.concatenate([sums[:, o], pick(w_st, my_c ^ o, 1), parts[:, 96:]], 1)

    both = jnp.stack(trade([c_piece(0), c_piece(1)], "core"))
    both = jnp.stack([pick(both, my_c, 0), pick(both, 1 - my_c, 0)])
    rows = natural(both.transpose(2, 1, 0, 3).reshape(80, 4, 2, 128), 80)
    node_grad = node_pass(rows[:32], cotan, w_source, w_target)
    rows = in_order(trade([jnp.concatenate([rows[32:], w_o])] * 4, "y"), my_y).astype(F32)
    grad_out = rows[:, 48:].reshape(2, 2, 16, 512).transpose(1, 2, 0, 3).reshape(32, 1024)
    return (
        node_grad[None],
        rows[:2, :16].reshape(32, 1024),
        rows[2:, :16].reshape(32, 1024),
        grad_out,
        rows[:, 16:48].reshape(128, 1024),
    )


def solution(mesh):
    fine = Mesh(mesh.devices.reshape(2, 4, 4, 4, 2), ("zlo", "y", "x", "zhi", "core"))
    dp, graph = ("zlo", "y"), ("x", "zhi", "core")
    placed = (
        P(dp, graph, None),
        P(dp, graph, None),
        P(dp, graph, None),
        P(dp, graph),
        P(dp, graph),
        P(dp, graph),
        P(),
        P(),
        P(),
        P(),
    )
    return jax.shard_map(
        per_device,
        mesh=fine,
        in_specs=placed,
        out_specs=(
            P(dp, graph, None),
            P(graph, None),
            P(graph, None),
            P(graph, None),
            P(),
        ),
        check_vma=False,
    )
```

```python
import jax
import jax.numpy as jnp
from jax import lax
from jax.experimental import pallas as pl
from jax.experimental.pallas import tpu as pltpu
from jax.sharding import Mesh
from jax.sharding import PartitionSpec as P

BF = jnp.bfloat16
F32 = jnp.float32


def dot(left, right, dims=((1,), (0,))):
    return lax.dot_general(left, right, (dims, ((), ())), preferred_element_type=F32)


def pick(array, index, axis):
    return lax.dynamic_index_in_dim(array, index, axis, keepdims=False)


def send(array, axis, offset):
    size = lax.axis_size(axis)
    return lax.ppermute(array, axis, [(i, (i + offset) % size) for i in range(size)])


def gather_from(array, axis):
    return [array] + [send(array, axis, -o) for o in range(1, lax.axis_size(axis))]


def trade(pieces, axis):
    return [pieces[0]] + [send(pieces[o], axis, o) for o in range(1, len(pieces))]


def total(parts):
    out = parts[0].astype(F32)
    for part in parts[1:]:
        out = out + part.astype(F32)
    return out


def in_order(parts, me):
    size = len(parts)
    stacked = jnp.stack(parts)
    return jnp.stack([pick(stacked, (me - a) % size, 0) for a in range(size)])


def natural(array, lead):
    return array.reshape(lead, 4, 2, 4, 32).transpose(0, 1, 3, 2, 4).reshape(lead, 1024)


def edge_blocks(at_ref, refs, p_s, p_tq, w_r, acc_s, acc_t, acc_r):
    my_y, my_x, my_z, my_c = (at_ref[i] for i in range(4))
    spot = lax.broadcasted_iota(jnp.int32, (512, 768), 0).astype(jnp.int16)

    for i in range(4):
        edges = refs[i % 2][i // 2]
        radial = edges[:768]
        coded = edges[768:].astype(F32)
        node = (coded[:12] * 16.0 + coded[12:24]).astype(jnp.int32) - 1
        far_z = ((node >> 5) - my_z) & 3
        far_x = ((node >> 7) - my_x) & 3
        far_c = ((node >> 4) & 1) ^ my_c
        place = (far_c * 16 + far_x * 4 + far_z) * 16 + (node & 15)
        place = jnp.where(node >= 0, place, -1)

        def hot(first):
            row = jnp.concatenate([place[first + i : first + i + 1] for i in range(6)], axis=1)
            return jnp.where(spot == row.astype(jnp.int16), BF(1), BF(0))

        hot_s, hot_t = hot(0), hot(6)
        col = place.T
        spot_n = lax.broadcasted_iota(jnp.int32, (768, 512), 1).astype(jnp.int16)

        def hot_n(first):
            column = jnp.concatenate([col[:, first + i : first + i + 1] for i in range(6)], axis=0)
            return jnp.where(spot_n == jnp.broadcast_to(column, (768, 512)).astype(jnp.int16), BF(1), BF(0))

        both = dot(p_tq[...], hot_t)
        pre = dot(p_s[...], hot_s) + both[:128]
        gmsg = both[128:]
        rad = dot(w_r[...], radial, ((1,), (1,)))
        sig = 1.0 / (1.0 + jnp.exp(-pre))
        act = pre * sig
        message = (act * rad).astype(BF)
        grad_rad = (gmsg * act).astype(BF)
        grad_pre = (gmsg * rad * (sig + act * (1.0 - sig))).astype(BF)
        acc_t[...] += dot(jnp.concatenate([message, grad_pre]), hot_n(6))
        acc_s[...] += dot(grad_pre, hot_n(0))
        acc_r[...] += dot(grad_rad, radial)


def first_kernel(
    at_ref, mine_ref, sib_ref, edge_ref, edge_sib_ref, ws, wt, wo, wr,
    embed, cotan, p_s, p_tq, w_r, acc_s, acc_t, acc_r
):
    my_c = at_ref[3]

    def own(rows):
        parts = rows.reshape(4, 2, 32, rows.shape[1])
        return jnp.where(my_c == 0, parts[:, 0], parts[:, 1]).reshape(128, rows.shape[1])

    for half, ref in enumerate((mine_ref, sib_ref)):
        rows = pl.ds(half * 256, 256)
        embed[rows] = ref[:, :, 0].reshape(256, 1024)
        cotan[rows] = ref[:, :, 1].reshape(256, 1024)
    acc_s[...] = jnp.zeros_like(acc_s)
    acc_t[...] = jnp.zeros_like(acc_t)
    acc_r[...] = jnp.zeros_like(acc_r)
    p_s[...] = own(dot(embed[...], ws[...]).T).astype(BF)
    p_tq[:128] = own(dot(embed[...], wt[...]).T).astype(BF)
    p_tq[128:] = dot(own(wo[...]), cotan[...], ((1,), (1,))).astype(BF)
    w_r[...] = own(wr[...].astype(F32).T).astype(BF)
    edge_blocks(at_ref, (edge_ref, edge_sib_ref), p_s, p_tq, w_r, acc_s, acc_t, acc_r)


def second_kernel(
    at_ref, edge_ref, edge_sib_ref, embed, cotan, p_s, p_tq, w_r, in_s, in_t, in_r, *refs
):
    sums_refs, grad_refs = refs[:4], refs[4:8]
    grads_ref, acc_s, acc_t, acc_r = refs[8:]
    my_y, my_x, my_z, my_c = (at_ref[i] for i in range(4))
    acc_s[...] = in_s[...]
    acc_t[...] = in_t[...]
    acc_r[...] = in_r[...]
    edge_blocks(at_ref, (edge_ref, edge_sib_ref), p_s, p_tq, w_r, acc_s, acc_t, acc_r)

    for mat, flat in enumerate((acc_s[...], acc_t[128:])):
        nodes = flat.T.astype(BF)
        for c in range(2):
            for x in range(4):
                for z in range(4):
                    first = (c * 16 + x * 4 + z) * 16
                    sums_refs[z][x, c, mat] = nodes[first : first + 16]
        grad = dot(flat.astype(BF), embed[...]).T.astype(BF)
        for h in range(2):
            to = (2 * mat + h - my_y) & 3
            for i in range(32):
                grads_ref[to, i * 16 : i * 16 + 16] = grad[i * 32 + h * 16 : i * 32 + h * 16 + 16]
    grad = dot(acc_t[:128].astype(BF), cotan[...]).astype(BF)
    for k in range(2):
        for h in range(2):
            to = (2 * k + h - my_y) & 3
            for z in range(4):
                for b in range(4):
                    first, at = z * 32 + h * 16, 512 + (z * 4 + b) * 16
                    cols = slice(k * 512 + b * 128, k * 512 + b * 128 + 128)
                    grads_ref[to, at : at + 16] = grad[first : first + 16, cols]
    grad = acc_r[...].T.astype(BF)
    for y in range(4):
        grads_ref[(y - my_y) & 3, 768:800] = grad[y * 32 : y * 32 + 32]
    for o in range(4):
        grad_refs[o][...] = grads_ref[o]


def edge_pass(at, mine, sib, early, early_sib, late, late_sib, ws, wt, wo, wr):
    smem = pl.BlockSpec(memory_space=pltpu.SMEM)
    vmem = pl.BlockSpec(memory_space=pltpu.VMEM)
    half = pl.CostEstimate(
        flops=3_000_000_000, bytes_accessed=4_000_000, transcendentals=800_000
    )
    accumulators = [
        jax.ShapeDtypeStruct((128, 512), F32),
        jax.ShapeDtypeStruct((256, 512), F32),
        jax.ShapeDtypeStruct((128, 128), F32),
    ]
    state = pl.pallas_call(
        first_kernel,
        in_specs=[smem] + [vmem] * 8,
        out_specs=[vmem] * 8,
        out_shape=[
            jax.ShapeDtypeStruct((512, 1024), BF),
            jax.ShapeDtypeStruct((512, 1024), BF),
            jax.ShapeDtypeStruct((128, 512), BF),
            jax.ShapeDtypeStruct((256, 512), BF),
            jax.ShapeDtypeStruct((128, 128), BF),
        ]
        + accumulators,
        compiler_params=pltpu.CompilerParams(vmem_limit_bytes=16 * 1024 * 1024),
        cost_estimate=half,
    )(at, mine, sib, early, early_sib, ws, wt, wo, wr)
    return pl.pallas_call(
        second_kernel,
        in_specs=[smem] + [vmem] * 10,
        out_specs=[vmem] * 8,
        out_shape=[jax.ShapeDtypeStruct((4, 2, 2, 16, 128), BF)] * 4
        + [jax.ShapeDtypeStruct((800, 128), BF)] * 4,
        scratch_shapes=[pltpu.VMEM((4, 800, 128), BF)]
        + [pltpu.VMEM(leaf.shape, leaf.dtype) for leaf in accumulators],
        compiler_params=pltpu.CompilerParams(vmem_limit_bytes=16 * 1024 * 1024),
        cost_estimate=half,
    )(at, late, late_sib, *state)


def node_kernel(sums_ref, start_ref, w_ref, out_ref):
    push = dot(w_ref[...], sums_ref[...], ((1,), (1,)))
    out_ref[...] = start_ref[...].astype(F32) + push.T


def node_pass(sums, start, weight):
    vmem = pl.BlockSpec(memory_space=pltpu.VMEM)
    return pl.pallas_call(
        node_kernel,
        in_specs=[vmem] * 3,
        out_specs=vmem,
        out_shape=jax.ShapeDtypeStruct((16, 1024), F32),
        compiler_params=pltpu.CompilerParams(vmem_limit_bytes=8 * 1024 * 1024),
        cost_estimate=pl.CostEstimate(flops=35_000_000, bytes_accessed=2_200_000, transcendentals=0),
    )(sums, start, weight)


def per_device(
    node_embed, node_cotan, radial, source, target, edge_count, w_source, w_target, w_out, w_radial
):
    my_y, my_x = lax.axis_index("y"), lax.axis_index("x")
    my_z, my_c = lax.axis_index("zhi"), lax.axis_index("core")
    cotan = node_cotan[0]

    nodes = gather_from(jnp.concatenate([node_embed[0], cotan]).reshape(2, 16, 1024), "zhi")

    live = jnp.arange(768, dtype=jnp.int32) < edge_count[0, 0]
    ids = jnp.where(live[None], jnp.stack([source[0], target[0]]) + 1, 0)
    ids = jnp.stack([ids >> 4, ids & 15]).astype(BF).reshape(24, 128)
    edges = jnp.concatenate([radial[0], ids, jnp.zeros((8, 128), BF)])
    edges = gather_from(edges, "x")
    early, late = jnp.stack([edges[0], edges[2]]), jnp.stack([edges[1], edges[3]])
    early_sib = send(early, "core", 1)
    nodes = jnp.stack(gather_from(jnp.stack(nodes), "x"))

    def mine(weight, axis):
        return lax.dynamic_slice_in_dim(weight, my_x * 256, 256, axis)

    weights = (mine(w_source, 1), mine(w_target, 1), mine(w_out, 0), mine(w_radial, 1))
    nodes, late, early_sib = lax.optimization_barrier((nodes, late, early_sib))
    node_sib = send(nodes, "core", 1)
    late_sib = send(late, "core", 1)
    at = jnp.stack([my_y, my_x, my_z, my_c]).astype(jnp.int32)
    out = edge_pass(at, nodes, node_sib, early, early_sib, late, late_sib, *weights)
    sums, grads = out[:4], out[4:]

    y_parts = trade(grads, "y")
    sums = trade(sums, "zhi")
    summed = total(y_parts).astype(BF)
    w_st = summed[:512].reshape(4, 4, 2, 16, 128)
    w_o = summed[512:768].reshape(4, 64, 128)
    w_r = summed[768:]

    def z_piece(o):
        at = (my_z + o) & 3
        return jnp.concatenate([pick(w_st, at, 1).reshape(128, 128), pick(w_o, at, 0), w_r])

    parts = trade([z_piece(o) for o in range(4)], "zhi")
    parts, sums = lax.optimization_barrier((parts, sums))
    sums = total(sums).astype(BF).reshape(4, 64, 128)
    radial_part = total([in_order([p[192:] for p in parts], my_z)[a] for a in range(4)])
    summed = jnp.concatenate([total([p[:192] for p in parts]), radial_part]).astype(BF)
    summed = total(gather_from(summed, "zlo")).astype(BF)
    w_st = summed[:128].reshape(4, 32, 128)
    w_o = summed[128:192].reshape(4, 16, 128).transpose(1, 0, 2).reshape(8, 1024)
    w_r = summed[192:]

    parts = [jnp.concatenate([sums[o], pick(w_st, (my_x + o) & 3, 0), w_r]) for o in range(4)]
    parts = in_order(trade(parts, "x"), my_x)
    sums, w_st = parts[:, :64].reshape(4, 2, 32, 128), parts[:, 64:96].reshape(4, 2, 16, 128)

    def c_piece(o):
        return jnp.concatenate([sums[:, o], pick(w_st, my_c ^ o, 1), parts[:, 96:]], 1)

    both = jnp.stack(trade([c_piece(0), c_piece(1)], "core"))
    both = jnp.stack([pick(both, my_c, 0), pick(both, 1 - my_c, 0)])
    rows = natural(both.transpose(2, 1, 0, 3).reshape(80, 4, 2, 128), 80)
    node_grad = node_pass(rows[:16], cotan, w_source)
    node_grad = node_pass(rows[16:32], node_grad, w_target)
    rows = in_order(trade([jnp.concatenate([rows[32:], w_o])] * 4, "y"), my_y).astype(F32)
    grad_out = rows[:, 48:].reshape(2, 2, 16, 512).transpose(1, 2, 0, 3).reshape(32, 1024)
    return (
        node_grad[None],
        rows[:2, :16].reshape(32, 1024),
        rows[2:, :16].reshape(32, 1024),
        grad_out,
        rows[:, 16:48].reshape(128, 1024),
    )


def solution(mesh):
    fine = Mesh(mesh.devices.reshape(2, 4, 4, 4, 2), ("zlo", "y", "x", "zhi", "core"))
    dp, graph = ("zlo", "y"), ("x", "zhi", "core")
    placed = (
        P(dp, graph, None),
        P(dp, graph, None),
        P(dp, graph, None),
        P(dp, graph),
        P(dp, graph),
        P(dp, graph),
        P(),
        P(),
        P(),
        P(),
    )
    return jax.shard_map(
        per_device,
        mesh=fine,
        in_specs=placed,
        out_specs=(
            P(dp, graph, None),
            P(graph, None),
            P(graph, None),
            P(graph, None),
            P(),
        ),
        check_vma=False,
    )
```
